32 devices in a mesh: groups: 2 (over y), ctx: 16 (over z, x, core).
Axes of the slice: x: 2, y: 2, z: 4, core: 2. Of those that a mesh axis runs over, the one named last changes fastest.
Arguments:
- hidden: bfloat16 [16384, 7168], P(('groups', 'ctx')), parts along dimension 0, may hold values from -6 to 6
- attn_gain: bfloat16 [7168], replicated, may hold values from 0.099609375 to 1.8984375
- w_dkv: bfloat16 [7168, 576], replicated, may hold values from -0.0625 to 0.0625
- kv_gain: bfloat16 [512], replicated, may hold values from 0.099609375 to 1.8984375
- lengths: int32 [8], P('groups'), parts along dimension 0, may hold values from 1 to 384, 512 in all
- owners: int32 [8], P('groups'), parts along dimension 0, may hold values from 0 to 3, each once
- queries: bfloat16 [8, 4, 128, 576], P('groups'), parts along dimension 0, may hold values from -60 to 60
- step_rows: bfloat16 [8, 4, 576], P('groups'), parts along dimension 0, may hold values from -12 to 12
Outputs:
- attended: bfloat16 [8, 4, 128, 512], P('groups', None, 'ctx'), parts along dimension 0
The draws below stay inside these ranges and needn't reach their ends.
There are 2 independent parts, one for each index of `groups`. The reference program is written for one: setup_inputs(seed, part) draws one part's arguments, and reference() takes and returns one part's arrays. A program takes and returns all parts, laid end to end along the dimension named above; an argument that names none is the same for every part. Nothing has to cross between parts.
Inputs may be any that keep to these rules, and one draw needn't show every extreme that they name: `lengths`: each request's prompt holds 16 times its entry rows, that many on every ctx device; some entry equals 384. `owners`: every block of 4 devices decodes exactly one request.
All inputs are finite; a program needn't handle non-finite values.
Results may differ from the reference program's by a relative error of at most 0.0064.
Values may be sent and summed in bfloat16 or wider, within the bound.
No kernel may reach another device: no remote copies, remote signals or barrier semaphores. Data moves between devices by JAX's collectives and lax.ppermute only.
A program may use at most 128 MiB of HBM per device.

```python
import math
import jax
import jax.numpy as jnp
import numpy as np
from jax import lax

D = 7168
H = 128
KVL = 512
ROPE = 64
NOPE = 128
PTOK = 512
STEPS = 4
REQS = 4
OWN = 4
TOKENS = 8192
MOSTL = 384
CAP = 96
N_CTX = 16


def draw_hidden(key, part):
    key = jax.random.fold_in(key, 7)
    noise_key = jax.random.fold_in(key, 0)
    values = jnp.clip(jax.random.normal(noise_key, (TOKENS, D), jnp.float32), -6.0, 6.0)
    return values.astype(jnp.bfloat16)


def draw_queries(key, part):
    key = jax.random.fold_in(key, 5)
    base_key = jax.random.fold_in(key, 0)
    base = jax.random.normal(base_key, (REQS, STEPS, H, KVL + ROPE), jnp.float32)
    values = jnp.clip(base, -6.0, 6.0)
    return values.astype(jnp.bfloat16)


def split_up(number_of, total, reach, skew):
    portions = [(1 << 20) // math.isqrt(standing ** skew) + 1 for standing in range(2, number_of + 1)]
    spare, given = total - reach - (number_of - 1), [1] * (number_of - 1)
    while spare > 0:
        candidates = [i for i in range(number_of - 1) if given[i] < reach]
        whole, remaining = sum([portions[i] for i in candidates]), spare
        for i in candidates:
            more = min(reach - given[i], max(1, remaining * portions[i] // whole), spare)
            given[i] = given[i] + more
            spare = spare - more
    return np.array([reach] + given)


def uneven(rng, number_of, total, reach, lean):
    if number_of == 2:
        one = jax.random.randint(rng, (), max(1, total - reach), min(reach, total - 1) + 1)
        return jnp.stack([one, total - one])
    sizes = jnp.asarray(split_up(number_of, total, reach, lean), jnp.int32)
    twos = (number_of - 1) // 2
    source_of, receiver = sizes[1:1 + 2 * twos:2], sizes[2:2 + 2 * twos:2]
    room = jnp.minimum(source_of - 1, reach - receiver)
    passed = jax.random.randint(jax.random.fold_in(rng, 1), (twos,), 0, 1 << 20) % (room + 1)
    sizes = sizes.at[1:1 + 2 * twos:2].set(source_of - passed).at[2:2 + 2 * twos:2].set(receiver + passed)
    return sizes[jax.random.permutation(jax.random.fold_in(rng, 2), number_of)]


def scatter_about(stream_key, dims, scale, most, kind=jnp.bfloat16):
    entries = scale * jax.random.normal(stream_key, dims, jnp.float32)
    return jnp.clip(entries, min=-most, max=most).astype(kind)


def setup_inputs(seed: int = 0, part: int = 0) -> dict:
    key_of = jax.random.split(jax.random.key(seed), 9)
    part_splits = jax.random.split(jax.random.fold_in(key_of[8], part), 9)
    hidden = draw_hidden(jax.random.fold_in(jax.random.fold_in(key_of[8], part), 71), part)
    attn_gain = jnp.clip(1.0 + 0.18 * jax.random.normal(key_of[1], (D,), jnp.float32), 0.099609375, 1.8984375).astype(jnp.bfloat16)
    w_dkv = scatter_about(key_of[2], (D, KVL + ROPE), D ** -0.5, 0.0625)
    kv_gain = jnp.clip(1.0 + 0.18 * jax.random.normal(key_of[3], (KVL,), jnp.float32), 0.099609375, 1.8984375).astype(jnp.bfloat16)
    lengths = uneven(part_splits[4], REQS, PTOK, MOSTL, 2).astype(jnp.int32)
    owners = jax.random.permutation(part_splits[5], REQS).astype(jnp.int32)
    queries = draw_queries(jax.random.fold_in(jax.random.fold_in(key_of[8], part), 71), part)
    step_rows = scatter_about(part_splits[7], (REQS, STEPS, KVL + ROPE), 2.5, 12.0)
    return {"hidden": hidden, "attn_gain": attn_gain, "w_dkv": w_dkv, "kv_gain": kv_gain, "lengths": lengths, "owners": owners, "queries": queries, "step_rows": step_rows}


EPSILON = 1e-06

def compress(row_block, first_row, device, attn_gain, w_dkv, kv_gain, starts, lengths):
    values = row_block.astype(jnp.float32)
    meansq = lax.optimization_barrier(jnp.mean(values * values, axis=-1, keepdims=True))
    normed = (values * lax.rsqrt(meansq + EPSILON) * attn_gain.astype(jnp.float32)).astype(jnp.bfloat16)
    projected = jnp.dot(normed, w_dkv, preferred_element_type=jnp.float32)
    latent = projected[:, :KVL]
    latent_sq = lax.optimization_barrier(jnp.mean(latent * latent, axis=-1, keepdims=True))
    latent = latent * lax.rsqrt(latent_sq + EPSILON) * kv_gain.astype(jnp.float32)
    local_index = first_row + jnp.arange(row_block.shape[0], dtype=jnp.int32)
    end_rows = starts + lengths
    member = (local_index[:, None] >= starts[None, :]) & (local_index[:, None] < end_rows[None, :])
    row_start = lax.optimization_barrier(jnp.sum(jnp.where(member, starts[None, :], 0), axis=1))
    row_length = lax.optimization_barrier(jnp.sum(jnp.where(member, lengths[None, :], 0), axis=1))
    position = (device * row_length + local_index - row_start).astype(jnp.float32)
    half_rope = ROPE // 2
    frequency = 10000.0 ** (-2.0 * jnp.arange(half_rope, dtype=jnp.float32) / ROPE)
    angles = position[:, None] * frequency[None, :]
    cosine = jnp.cos(angles)
    sine_part = jnp.sin(angles)
    first_half = projected[:, KVL:KVL + half_rope]
    second_half = projected[:, KVL + half_rope:]
    rotated = jnp.concatenate([first_half * cosine - second_half * sine_part, second_half * cosine + first_half * sine_part], axis=-1)
    return jnp.concatenate([latent, rotated], axis=-1).astype(jnp.bfloat16)

def group_state(key_rows, key_valid, group, query_block, step_keys):
    step_count = query_block.shape[0]
    head_count = query_block.shape[1]
    flat_query = query_block.reshape(step_count * head_count, -1)
    every_key = jnp.concatenate([key_rows, step_keys], axis=0)
    scores = jnp.dot(flat_query, every_key.T, preferred_element_type=jnp.float32) * (NOPE + ROPE) ** (-0.5)
    query_step = jnp.arange(step_count * head_count, dtype=jnp.int32) // head_count
    causal = (jnp.arange(step_count, dtype=jnp.int32)[None, :] <= query_step[:, None]) & (group == 0)
    prompt_mask = jnp.broadcast_to(key_valid[None, :], (step_count * head_count, key_valid.shape[0]))
    allowed = jnp.concatenate([prompt_mask, causal], axis=1)
    scores = jnp.where(allowed, scores, -1e+30)
    group_peak = lax.optimization_barrier(jnp.max(scores, axis=1))
    exponent = jnp.where(allowed, jnp.exp(scores - group_peak[:, None]), 0.0)
    group_total = lax.optimization_barrier(jnp.sum(exponent, axis=1))
    weights = exponent.astype(jnp.bfloat16)
    part = jnp.dot(weights, every_key[:, :KVL], preferred_element_type=jnp.float32)
    return (group_peak, group_total, part)

def reference(hidden, attn_gain, w_dkv, kv_gain, lengths, owners, queries, step_rows):
    devices = N_CTX
    starts = (jnp.cumsum(lengths) - lengths).astype(jnp.int32)
    is_match = owners[None, :] == jnp.arange(REQS, dtype=jnp.int32)[:, None]
    block_request = lax.optimization_barrier(jnp.sum(jnp.where(is_match, jnp.arange(REQS, dtype=jnp.int32)[None, :], 0), axis=1)).astype(jnp.int32)
    shards = hidden.reshape(devices, PTOK, D)

    def per_device(item):
        row_block, device = item
        return compress(row_block, 0, device, attn_gain, w_dkv, kv_gain, starts, lengths)
    cache_rows = lax.map(per_device, (shards, jnp.arange(devices, dtype=jnp.int32)))

    def per_block(item):
        request, query_block, step_keys = item
        is_request = jnp.arange(REQS, dtype=jnp.int32) == request
        first = jnp.sum(jnp.where(is_request, starts, 0)).astype(jnp.int32)
        count_rows = jnp.sum(jnp.where(is_request, lengths, 0)).astype(jnp.int32)
        lanes = jnp.arange(OWN, dtype=jnp.int32)
        offsets = lanes[:, None] + OWN * jnp.arange(CAP, dtype=jnp.int32)[None, :]
        row_index = jnp.clip(first + offsets, 0, PTOK - 1).astype(jnp.int32)
        row_valid = offsets < count_rows

        def per_group(group_item):
            group, index_row, valid_row = group_item
            picked = jnp.take(cache_rows, index_row, axis=1).reshape(devices * CAP, KVL + ROPE)
            key_valid = jnp.broadcast_to(valid_row[None, :], (devices, CAP)).reshape(-1)
            return group_state(picked, key_valid, group, query_block, step_keys)
        peaks, totals, parts = lax.map(per_group, (lanes, row_index, row_valid))
        peak = lax.optimization_barrier(jnp.max(peaks, axis=0))
        scale = jnp.exp(peaks - peak[None, :])
        summed = lax.optimization_barrier(jnp.sum(parts * scale[:, :, None], axis=0))
        total = lax.optimization_barrier(jnp.sum(totals * scale, axis=0))
        mixture = summed / total[:, None]
        return mixture.reshape(STEPS, H, KVL).astype(jnp.bfloat16)
    return lax.map(per_block, (block_request, queries, step_rows))
```

```python
import functools
import math

import jax
import jax.numpy as jnp
import numpy as np
from jax import lax
from jax.experimental import pallas as pl
from jax.experimental.pallas import tpu as pltpu
from jax.sharding import PartitionSpec as P

KVL = 512
ROPE = 64
NOPE = 128
WIDTH = KVL + ROPE
EPSILON = 1e-06
SCALE = (NOPE + ROPE) ** (-0.5)
STAT_ROWS = 8
VMEM_BYTES = 48 * 1024 * 1024

NT = (((1,), (1,)), ((), ()))


def place(devices):
    cores = 2 if devices % 2 == 0 else 1
    chips = devices // cores
    along_x = max(k for k in range(1, chips + 1) if chips % k == 0 and k * k * k <= chips)
    return chips // along_x, along_x, cores


def scalars(lengths_ref, owners_ref, most):
    count = lengths_ref.shape[0]
    starts = []
    total = jnp.int32(0)
    for r in range(count):
        starts.append(total)
        total = total + lengths_ref[r]
    long_start, long_block = jnp.int32(0), jnp.int32(0)
    for r in range(count):
        is_long = lengths_ref[r] == most
        long_start = jnp.where(is_long, starts[r], long_start)
        long_block = jnp.where(is_long, owners_ref[r], long_block)
    return starts, long_start, long_block


def short_slots(lengths_ref, owners_ref, starts, long_block):
    count = lengths_ref.shape[0]
    slots = []
    for i in range(count - 1):
        block = jnp.where(long_block <= i, jnp.int32(i + 1), jnp.int32(i))
        first, rows = jnp.int32(0), jnp.int32(0)
        for r in range(count):
            is_it = owners_ref[r] == block
            first = jnp.where(is_it, starts[r], first)
            rows = jnp.where(is_it, lengths_ref[r], rows)
        slots.append((block, first, rows))
    return slots


def sin_cos(angle):
    n = jnp.round(angle * np.float32(2.0 / math.pi))
    r = ((angle - n * np.float32(1.5703125)) - n * np.float32(4.8375129699707031e-4)) - n * np.float32(
        7.5497899548918822e-8
    )
    z = r * r
    sine = ((np.float32(-1.9515295891e-4) * z + np.float32(8.3321608736e-3)) * z + np.float32(-1.6666654611e-1)) * z * r + r
    cosine = (
        ((np.float32(2.443315711809948e-5) * z + np.float32(-1.388731625493765e-3)) * z + np.float32(4.166664568298827e-2)) * z * z
        - np.float32(0.5) * z
        + np.float32(1.0)
    )
    quadrant = n.astype(jnp.int32) & 3
    odd = (quadrant & 1) == 1
    out_sine = jnp.where(odd, cosine, sine)
    out_cosine = jnp.where(odd, sine, cosine)
    out_sine = jnp.where(quadrant >= 2, -out_sine, out_sine)
    out_cosine = jnp.where((quadrant == 1) | (quadrant == 2), -out_cosine, out_cosine)
    return out_sine, out_cosine


def compress_kernel(
    most,
    chunks,
    lengths_hbm,
    owners_hbm,
    x_hbm,
    gain_hbm,
    w_hbm,
    kv_gain_hbm,
    long_ref,
    short_ref,
    x_buf,
    w_buf,
    acc,
    lengths_ref,
    owners_ref,
    gain_ref,
    kv_gain_ref,
    small,
    sem,
):
    tokens, model = x_buf.shape
    head = [
        pltpu.make_async_copy(source, target, small.at[i])
        for i, (source, target) in enumerate(
            ((lengths_hbm, lengths_ref), (owners_hbm, owners_ref), (gain_hbm, gain_ref), (kv_gain_hbm, kv_gain_ref))
        )
    ]
    copies, begin = [], 0
    for i, depth in enumerate(chunks):
        part = pl.ds(begin, depth)
        copies.append(
            (
                pltpu.make_async_copy(w_hbm.at[:, part], w_buf.at[:, part], sem.at[0, i]),
                pltpu.make_async_copy(x_hbm.at[:, part], x_buf.at[:, part], sem.at[1, i]),
            )
        )
        begin += depth
    for copy in head:
        copy.start()
    for pair in copies:
        for copy in pair:
            copy.start()
    for copy in head:
        copy.wait()

    device = lax.axis_index("ctx")
    starts, long_start, _ = scalars(lengths_ref, owners_ref, most)
    half = ROPE // 2
    token = lax.broadcasted_iota(jnp.int32, (1, tokens), 1)
    position = jnp.zeros((1, tokens), jnp.int32)
    for r in range(lengths_ref.shape[0]):
        inside = (token >= starts[r]) & (token < starts[r] + lengths_ref[r])
        position = jnp.where(inside, device * lengths_ref[r] + token - starts[r], position)
    index = lax.broadcasted_iota(jnp.int32, (half, 1), 0)
    frequency = jnp.zeros((half, 1), jnp.float32)
    for i in range(half):
        frequency = jnp.where(index == i, np.float32(10000.0 ** (-2.0 * i / ROPE)), frequency)
    sine, cosine = sin_cos(frequency * position.astype(jnp.float32))
    gain = jnp.transpose(jnp.broadcast_to(kv_gain_ref[...].astype(jnp.float32).reshape(1, KVL), (128, KVL)))
    row_gain = gain_ref[...].reshape(1, model)
    source = lax.broadcasted_iota(jnp.int32, (tokens, tokens), 0) + long_start
    source = jnp.where(source >= tokens, source - tokens, source)
    turn = (source == lax.broadcasted_iota(jnp.int32, (tokens, tokens), 1)).astype(jnp.bfloat16)

    squares = jnp.zeros((tokens, 128), jnp.float32)
    begin = 0
    for i, depth in enumerate(chunks):
        part = slice(begin, begin + depth)
        for copy in copies[i]:
            copy.wait()
        x = x_buf[:, part]
        product = lax.dot_general(w_buf[:, part], x * row_gain[:, part], NT, preferred_element_type=jnp.float32)
        if i == 0:
            acc[...] = product
        else:
            acc[...] += product
        for j in range(depth // 128):
            piece = x[:, j * 128 : (j + 1) * 128].astype(jnp.float32)
            squares = squares + piece * piece
        begin += depth
    mean = jnp.sum(jnp.transpose(squares), axis=0, keepdims=True) * np.float32(1.0 / model)
    scale = lax.rsqrt(mean + EPSILON)
    latent = acc[:KVL, :]
    latent_mean = jnp.sum(latent * latent, axis=0, keepdims=True) * (scale * scale) * np.float32(1.0 / KVL)
    latent = latent * (scale * lax.rsqrt(latent_mean + EPSILON)) * wide(gain, tokens)
    first = acc[KVL : KVL + half, :] * scale
    second = acc[KVL + half :, :] * scale
    columns = jnp.concatenate(
        [latent, first * cosine - second * sine, second * cosine + first * sine], axis=0
    ).astype(jnp.bfloat16)
    turned = lax.dot_general(turn, columns, NT, preferred_element_type=jnp.float32).astype(jnp.bfloat16)
    long_ref[...] = turned[:most]
    short_ref[...] = turned[most:]


def pick_kernel(most, sizes, lengths_ref, owners_ref, queries_hbm, long_ref, short_ref, buf, long_buf, short_buf, sem):
    zs, xs, cores = sizes
    device = lax.axis_index("ctx")
    _, _, long_block = scalars(lengths_ref, owners_ref, most)
    count, steps, _, heads = queries_hbm.shape
    local = heads // (zs * xs * cores)
    core = lax.rem(device, cores)
    here_x = lax.rem(device // cores, xs)
    here_z = device // (cores * xs)
    blocks = [long_block] + [jnp.where(long_block <= i, i + 1, i) for i in range(count - 1)]
    copies = [
        pltpu.make_async_copy(queries_hbm.at[block], buf.at[i], sem.at[i]) for i, block in enumerate(blocks)
    ]
    for copy in copies:
        copy.start()

    def head_of(rows, spread):
        row = lax.broadcasted_iota(jnp.int32, (rows, heads), 0)
        unit, inner = row // local, lax.rem(row, local)
        z = lax.rem(lax.rem(unit, zs) + here_z, zs)
        x = lax.rem(unit // zs + here_x, xs) if spread else here_x
        head = ((z * xs + x) * cores + core) * local + inner
        return (head == lax.broadcasted_iota(jnp.int32, (rows, heads), 1)).astype(jnp.bfloat16)

    long_pick, short_pick = head_of(xs * zs * local, True), head_of(zs * local, False)
    copies[0].wait()
    for t in range(steps):
        rows = lax.dot_general(long_pick, buf[0, t], NT, preferred_element_type=jnp.float32)
        for u in range(xs * zs):
            long_buf[(u * steps + t) * local : (u * steps + t + 1) * local, :] = rows[u * local : (u + 1) * local]
    long_ref[...] = long_buf[...].astype(jnp.bfloat16)
    for i in range(1, count):
        copies[i].wait()
        for t in range(steps):
            rows = lax.dot_general(short_pick, buf[i, t], NT, preferred_element_type=jnp.float32)
            for u in range(zs):
                at = ((u * (count - 1) + i - 1) * steps + t) * local
                short_buf[at : at + local, :] = rows[u * local : (u + 1) * local]
    short_ref[...] = short_buf[...].astype(jnp.bfloat16)


def as_line(column):
    return jnp.transpose(jnp.broadcast_to(column, (column.shape[0], 128)))[:8]


def as_columns(line):
    return jnp.transpose(jnp.broadcast_to(line, (128, line.shape[1])))


def stat_rows(line):
    rows = line.shape[1]
    high = line.astype(jnp.bfloat16).astype(jnp.float32)
    rest = line - high
    middle = rest.astype(jnp.bfloat16).astype(jnp.float32)
    low = rest - middle
    index = lax.broadcasted_iota(jnp.int32, (STAT_ROWS, rows), 0)
    pieces = jnp.where(index == 0, high, jnp.where(index == 1, middle, jnp.where(index == 2, low, 0.0)))
    if rows < KVL:
        pieces = jnp.concatenate([pieces, jnp.zeros((STAT_ROWS, KVL - rows), jnp.float32)], axis=1)
    return pieces


def read_line(pieces, rows):
    return pieces[0:1, :rows] + pieces[1:2, :rows] + pieces[2:3, :rows]


def wide(stat, width=KVL):
    return jnp.concatenate([stat] * (width // 128), axis=1)


def long_kernel(q_ref, key_refs, out_refs):
    keys = jnp.concatenate([ref[...] for ref in key_refs], axis=0)
    rows = q_ref.shape[0] // len(out_refs)
    scores = lax.dot_general(q_ref[...], keys, NT, preferred_element_type=jnp.float32) * SCALE
    peak = jnp.max(scores, axis=1, keepdims=True)
    weights = jnp.exp(scores - peak)
    total = jnp.sum(weights, axis=1, keepdims=True)
    mixed = jnp.dot(weights.astype(jnp.bfloat16), keys[:, :KVL], preferred_element_type=jnp.float32) / total
    lse = peak + jnp.log(total)
    for j, ref in enumerate(out_refs):
        part = slice(j * rows, (j + 1) * rows)
        ref[...] = jnp.concatenate([mixed[part], stat_rows(as_line(lse[part]))], axis=0).astype(jnp.bfloat16)


def short_kernel(most, lengths_ref, owners_ref, q_ref, key_refs, out_refs, lse_ref):
    count = lengths_ref.shape[0]
    starts, long_start, long_block = scalars(lengths_ref, owners_ref, most)
    slots = short_slots(lengths_ref, owners_ref, starts, long_block)
    keys = jnp.concatenate([ref[...] for ref in key_refs], axis=0)
    shorts = key_refs[0].shape[0]
    tokens = shorts + most
    rows = q_ref.shape[0]
    per_dest = rows // len(out_refs)
    per_slot = per_dest // (count - 1)
    scores = lax.dot_general(q_ref[...], keys, NT, preferred_element_type=jnp.float32) * SCALE
    key = lax.rem(lax.broadcasted_iota(jnp.int32, (1, keys.shape[0]), 1), shorts)
    local = key + (long_start + most)
    local = jnp.where(local >= tokens, local - tokens, local)
    slot = lax.rem(lax.broadcasted_iota(jnp.int32, (rows, 1), 0), per_dest) // per_slot
    first, stop = jnp.zeros_like(slot), jnp.zeros_like(slot)
    for i, (_, start, length) in enumerate(slots):
        first = jnp.where(slot == i, start, first)
        stop = jnp.where(slot == i, start + length, stop)
    allowed = (local >= first) & (local < stop)
    scores = jnp.where(allowed, scores, -1e30)
    peak = jnp.max(scores, axis=1, keepdims=True)
    weights = jnp.where(allowed, jnp.exp(scores - peak), 0.0)
    total = jnp.sum(weights, axis=1, keepdims=True)
    mixed = jnp.dot(weights.astype(jnp.bfloat16), keys[:, :KVL], preferred_element_type=jnp.float32) / total
    lse = peak + jnp.log(total)
    for k, ref in enumerate(out_refs):
        part = slice(k * per_dest, (k + 1) * per_dest)
        ref[...] = mixed[part].astype(jnp.bfloat16)
        lse_ref[k] = as_line(lse[part])


def merge_kernel(part_refs, lse_ref, out_refs):
    rows = part_refs[0].shape[0] - STAT_ROWS
    per_dest = rows // len(out_refs)
    parts = [ref[...].astype(jnp.float32) for ref in part_refs]
    lines = [read_line(part[rows:], rows) for part in parts]
    top = functools.reduce(jnp.maximum, lines)
    shares = [jnp.exp(line - top) for line in lines]
    whole = functools.reduce(lambda a, b: a + b, shares)
    mixed = functools.reduce(
        lambda a, b: a + b, [wide(as_columns(share / whole)) * part[:rows] for share, part in zip(shares, parts)]
    )
    lse = jnp.broadcast_to(top + jnp.log(whole), (8, rows))
    for k, ref in enumerate(out_refs):
        part = slice(k * per_dest, (k + 1) * per_dest)
        both = jnp.concatenate([lse_ref[k], lse[:, part]], axis=1)
        ref[...] = jnp.concatenate([mixed[part], stat_rows(both)], axis=0).astype(jnp.bfloat16)


def step_kernel(most, steps, lengths_ref, owners_ref, long_q_ref, short_q_ref, step_ref, after_ref, out_ref, lse_ref):
    count = lengths_ref.shape[0]
    _, _, long_block = scalars(lengths_ref, owners_ref, most)
    blocks = [jnp.where(long_block <= i, i + 1, i) for i in range(count - 1)] + [long_block]
    rows = out_ref.shape[0]
    per_slot = rows // count
    heads = per_slot // steps
    query = jnp.concatenate(
        [short_q_ref[: rows - per_slot, :].astype(jnp.float32), long_q_ref[:per_slot, :].astype(jnp.float32)], axis=0
    ).astype(jnp.bfloat16)
    keys = jnp.concatenate([step_ref[b].astype(jnp.float32) for b in blocks], axis=0).astype(jnp.bfloat16)
    scores = lax.dot_general(query, keys, NT, preferred_element_type=jnp.float32) * SCALE
    row = lax.broadcasted_iota(jnp.int32, scores.shape, 0)
    column = lax.broadcasted_iota(jnp.int32, scores.shape, 1)
    allowed = (row // per_slot == column // steps) & (lax.rem(column, steps) <= lax.rem(row, per_slot) // heads)
    scores = jnp.where(allowed, scores, -1e30)
    peak = jnp.max(scores, axis=1, keepdims=True)
    weights = jnp.where(allowed, jnp.exp(scores - peak), 0.0)
    total = jnp.sum(weights, axis=1, keepdims=True)
    out_ref[...] = jnp.dot(weights.astype(jnp.bfloat16), keys[:, :KVL], preferred_element_type=jnp.float32) / total
    lse_ref[...] = as_line(peak + jnp.log(total))


def last_kernel(most, lengths_ref, owners_ref, step_ref, step_lse_ref, short_refs, long_refs, out_ref):
    count = lengths_ref.shape[0]
    _, _, long_block = scalars(lengths_ref, owners_ref, most)
    blocks = [jnp.where(long_block <= i, i + 1, i) for i in range(count - 1)] + [long_block]
    rows, per_slot = step_ref.shape[0], long_refs[0].shape[0] - STAT_ROWS
    shorts = rows - per_slot
    longs = [ref[...].astype(jnp.float32) for ref in long_refs]
    lines = [step_lse_ref[:1]] + [read_line(part[per_slot:], rows) for part in longs]
    top = functools.reduce(jnp.maximum, lines)
    shares = [jnp.exp(line - top) for line in lines]
    whole = functools.reduce(lambda a, b: a + b, shares)
    columns = [wide(as_columns(share / whole)) for share in shares]
    step = step_ref[...]
    short, long = columns[0][:shorts] * step[:shorts], columns[0][shorts:] * step[shorts:]
    for column, ref, part in zip(columns[1:], short_refs, longs):
        short = short + column[:shorts] * ref[...].astype(jnp.float32)
        long = long + column[shorts:] * part[:per_slot]
    for i in range(count - 1):
        out_ref[blocks[i]] = short[i * per_slot : (i + 1) * per_slot].astype(jnp.bfloat16)
    out_ref[long_block] = long.astype(jnp.bfloat16)


SMEM = pl.BlockSpec(memory_space=pltpu.SMEM)
VMEM = pl.BlockSpec(memory_space=pltpu.VMEM)
HBM = pl.BlockSpec(memory_space=pl.ANY)


def params(**more):
    return pltpu.CompilerParams(vmem_limit_bytes=VMEM_BYTES, **more)


def shards(hidden, attn_gain, w_dkv, kv_gain, lengths, owners, queries, step_rows):
    devices = lax.axis_size("ctx")
    sizes = place(devices)
    zs, xs, cores = sizes
    tokens, model = hidden.shape
    count, steps, heads, _ = queries.shape
    most = min(3 * tokens // count, tokens - count + 1)
    shorts = tokens - most
    local = heads // devices
    bf16, f32 = jnp.bfloat16, jnp.float32

    def moved(dz, dx, dc):
        pairs = []
        for z in range(zs):
            for x in range(xs):
                for c in range(cores):
                    to = ((z + dz) % zs * xs + (x + dx) % xs) * cores + (c + dc) % cores
                    pairs.append(((z * xs + x) * cores + c, to))
        return pairs

    def send(value, dz=0, dx=0, dc=0):
        return lax.ppermute(value, "ctx", moved(dz, dx, dc))

    chunks = [1024] * ((model - 1024) // 1024)
    while sum(chunks) < model:
        chunks.append(min(512, model - sum(chunks)))
    long_keys, short_keys = pl.pallas_call(
        functools.partial(compress_kernel, most, chunks),
        in_specs=[HBM] * 6,
        out_specs=[VMEM, VMEM],
        out_shape=[jax.ShapeDtypeStruct((most, WIDTH), bf16), jax.ShapeDtypeStruct((shorts, WIDTH), bf16)],
        scratch_shapes=[
            pltpu.VMEM((tokens, model), bf16),
            pltpu.VMEM((WIDTH, model), bf16),
            pltpu.VMEM((WIDTH, tokens), f32),
            pltpu.SMEM(lengths.shape, lengths.dtype),
            pltpu.SMEM(owners.shape, owners.dtype),
            pltpu.VMEM(attn_gain.shape, bf16),
            pltpu.VMEM(kv_gain.shape, bf16),
            pltpu.SemaphoreType.DMA((4,)),
            pltpu.SemaphoreType.DMA((2, len(chunks))),
        ],
        compiler_params=pltpu.CompilerParams(vmem_limit_bytes=60 * 1024 * 1024),
        cost_estimate=pl.CostEstimate(
            flops=2 * tokens * model * WIDTH, bytes_accessed=2 * model * (tokens + WIDTH), transcendentals=0
        ),
        name="compress",
    )(lengths, owners, hidden, attn_gain, w_dkv.T, kv_gain)

    long_rows, short_rows = zs * xs * steps * local, zs * (count - 1) * steps * local
    long_q, short_q = pl.pallas_call(
        functools.partial(pick_kernel, most, sizes),
        in_specs=[SMEM, SMEM, HBM],
        out_specs=[VMEM, VMEM],
        out_shape=[jax.ShapeDtypeStruct((long_rows, WIDTH), bf16), jax.ShapeDtypeStruct((short_rows, WIDTH), bf16)],
        scratch_shapes=[
            pltpu.VMEM((count, steps, WIDTH, heads), bf16),
            pltpu.VMEM((long_rows, WIDTH), f32),
            pltpu.VMEM((short_rows, WIDTH), f32),
            pltpu.SemaphoreType.DMA((count,)),
        ],
        compiler_params=params(),
        cost_estimate=pl.CostEstimate(
            flops=2 * (long_rows + short_rows) * WIDTH * heads,
            bytes_accessed=2 * count * steps * WIDTH * heads,
            transcendentals=0,
        ),
        name="pick_queries",
    )(lengths, owners, queries.transpose(0, 1, 3, 2))

    short_in = [short_keys] + [send(short_keys, dx=j) for j in range(1, xs)]
    long_in = [long_keys] + [send(long_keys, dc=j) for j in range(1, cores)]
    x_rows = long_rows // xs + STAT_ROWS
    parts = pl.pallas_call(
        lambda q, *refs: long_kernel(q, refs[:cores], refs[cores:]),
        in_specs=[VMEM] * (1 + cores),
        out_specs=[VMEM] * xs,
        out_shape=[jax.ShapeDtypeStruct((x_rows, KVL), bf16)] * xs,
        compiler_params=params(),
        cost_estimate=pl.CostEstimate(
            flops=2 * long_rows * most * cores * (WIDTH + KVL), bytes_accessed=4 * most * WIDTH, transcendentals=0
        ),
        name="long_part",
    )(long_q, *long_in)
    sent = [send(parts[j], dx=j) for j in range(1, xs)]
    own, *short_in = lax.optimization_barrier((parts[0], *short_in))
    parts = [own] + sent
    short_in = short_in + [send(k, dc=j) for j in range(1, cores) for k in short_in]

    per_short, per_long = short_rows // zs, long_rows // xs // zs
    *short_parts, short_lse = pl.pallas_call(
        lambda a, b, q, *refs: short_kernel(
            most, a, b, q, refs[: len(short_in)], refs[len(short_in) : len(short_in) + zs], refs[-1]
        ),
        in_specs=[SMEM, SMEM] + [VMEM] * (1 + len(short_in)),
        out_specs=[VMEM] * (zs + 1),
        out_shape=[jax.ShapeDtypeStruct((per_short, KVL), bf16)] * zs + [jax.ShapeDtypeStruct((zs, 8, per_short), f32)],
        compiler_params=params(),
        cost_estimate=pl.CostEstimate(
            flops=2 * short_rows * shorts * len(short_in) * (WIDTH + KVL),
            bytes_accessed=4 * shorts * len(short_in) * WIDTH,
            transcendentals=0,
        ),
        name="short_part",
    )(lengths, owners, short_q, *short_in)
    short_parts = [short_parts[0]] + [send(short_parts[k], dz=k) for k in range(1, zs)]

    long_parts = pl.pallas_call(
        lambda *refs: merge_kernel(refs[:xs], refs[xs], refs[xs + 1 :]),
        in_specs=[VMEM] * (xs + 1),
        out_specs=[VMEM] * zs,
        out_shape=[jax.ShapeDtypeStruct((per_long + STAT_ROWS, KVL), bf16)] * zs,
        compiler_params=params(),
        cost_estimate=pl.CostEstimate(flops=0, bytes_accessed=2 * xs * x_rows * KVL, transcendentals=0),
        name="long_merge",
    )(*parts, short_lse)
    after = long_parts[0]
    long_parts = [after] + [send(long_parts[k], dz=k) for k in range(1, zs)]

    rows = per_short + per_long
    step_part, step_lse = pl.pallas_call(
        functools.partial(step_kernel, most, steps),
        in_specs=[SMEM, SMEM, VMEM, VMEM, VMEM, HBM],
        out_specs=[VMEM, VMEM],
        out_shape=[jax.ShapeDtypeStruct((rows, KVL), f32), jax.ShapeDtypeStruct((8, rows), f32)],
        compiler_params=params(),
        cost_estimate=pl.CostEstimate(flops=0, bytes_accessed=4 * rows * KVL, transcendentals=0),
        name="step_part",
    )(lengths, owners, long_q, short_q, step_rows, after)

    out = pl.pallas_call(
        lambda a, b, s, l, *refs: last_kernel(most, a, b, s, l, refs[:zs], refs[zs : 2 * zs], refs[2 * zs]),
        in_specs=[SMEM, SMEM] + [VMEM] * (2 + 2 * zs),
        out_specs=VMEM,
        out_shape=jax.ShapeDtypeStruct((count, steps * local, KVL), bf16),
        compiler_params=params(),
        cost_estimate=pl.CostEstimate(flops=0, bytes_accessed=2 * zs * rows * KVL, transcendentals=0),
        name="combine",
    )(lengths, owners, step_part, step_lse, *short_parts, *long_parts)
    return out.reshape(count, steps, local, KVL)


def solution(mesh):
    in_specs = (
        P(("groups", "ctx"), None),
        P(),
        P(),
        P(),
        P("groups"),
        P("groups"),
        P("groups", None, None, None),
        P("groups", None, None),
    )
    out_specs = P("groups", None, "ctx", None)
    return jax.shard_map(shards, mesh=mesh, in_specs=in_specs, out_specs=out_specs, check_vma=False)
```

```python
import functools
import math

import jax
import jax.numpy as jnp
import numpy as np
from jax import lax
from jax.experimental import pallas as pl
from jax.experimental.pallas import tpu as pltpu
from jax.sharding import PartitionSpec as P

KVL = 512
ROPE = 64
NOPE = 128
WIDTH = KVL + ROPE
EPSILON = 1e-06
SCALE = (NOPE + ROPE) ** (-0.5)
STAT_ROWS = 8
PACK = KVL // ROPE
VMEM_BYTES = 48 * 1024 * 1024

NT = (((1,), (1,)), ((), ()))


def place(devices):
    cores = 2 if devices % 2 == 0 else 1
    chips = devices // cores
    along_x = max(k for k in range(1, chips + 1) if chips % k == 0 and k * k * k <= chips)
    return chips // along_x, along_x, cores


def scalars(lengths_ref, owners_ref, most):
    count = lengths_ref.shape[0]
    starts = []
    total = jnp.int32(0)
    for r in range(count):
        starts.append(total)
        total = total + lengths_ref[r]
    long_start, long_block = jnp.int32(0), jnp.int32(0)
    for r in range(count):
        is_long = lengths_ref[r] == most
        long_start = jnp.where(is_long, starts[r], long_start)
        if owners_ref is not None:
            long_block = jnp.where(is_long, owners_ref[r], long_block)
    return starts, long_start, long_block


def short_slots(lengths_ref, owners_ref, starts, long_block):
    count = lengths_ref.shape[0]
    slots = []
    for i in range(count - 1):
        block = jnp.where(long_block <= i, jnp.int32(i + 1), jnp.int32(i))
        first, rows = jnp.int32(0), jnp.int32(0)
        for r in range(count):
            is_it = owners_ref[r] == block
            first = jnp.where(is_it, starts[r], first)
            rows = jnp.where(is_it, lengths_ref[r], rows)
        slots.append((block, first, rows))
    return slots


def sin_cos(angle):
    n = jnp.round(angle * np.float32(2.0 / math.pi))
    r = ((angle - n * np.float32(1.5703125)) - n * np.float32(4.8375129699707031e-4)) - n * np.float32(
        7.5497899548918822e-8
    )
    z = r * r
    sine = ((np.float32(-1.9515295891e-4) * z + np.float32(8.3321608736e-3)) * z + np.float32(-1.6666654611e-1)) * z * r + r
    cosine = (
        ((np.float32(2.443315711809948e-5) * z + np.float32(-1.388731625493765e-3)) * z + np.float32(4.166664568298827e-2)) * z * z
        - np.float32(0.5) * z
        + np.float32(1.0)
    )
    quadrant = n.astype(jnp.int32) & 3
    odd = (quadrant & 1) == 1
    out_sine = jnp.where(odd, cosine, sine)
    out_cosine = jnp.where(odd, sine, cosine)
    out_sine = jnp.where(quadrant >= 2, -out_sine, out_sine)
    out_cosine = jnp.where((quadrant == 1) | (quadrant == 2), -out_cosine, out_cosine)
    return out_sine, out_cosine


def compress_kernel(
    most,
    chunks,
    lengths_hbm,
    x_hbm,
    gain_hbm,
    w_hbm,
    kv_gain_hbm,
    rows_ref,
    short_ref,
    x_buf,
    w_buf,
    acc,
    lengths_ref,
    gain_ref,
    kv_gain_ref,
    small,
    sem,
):
    tokens, model = x_buf.shape
    head = [
        pltpu.make_async_copy(source, target, small.at[i])
        for i, (source, target) in enumerate(
            ((lengths_hbm, lengths_ref), (gain_hbm, gain_ref), (kv_gain_hbm, kv_gain_ref))
        )
    ]
    copies, begin = [], 0
    for i, depth in enumerate(chunks):
        part = pl.ds(begin, depth)
        copies.append(
            (
                pltpu.make_async_copy(w_hbm.at[:, part], w_buf.at[:, part], sem.at[0, i]),
                pltpu.make_async_copy(x_hbm.at[:, part], x_buf.at[:, part], sem.at[1, i]),
            )
        )
        begin += depth
    for copy in head:
        copy.start()
    for copy in copies[0] + copies[1]:
        copy.start()
    for copy in head:
        copy.wait()
    for pair in copies[2:]:
        for copy in pair:
            copy.start()

    device = lax.axis_index("ctx")
    starts, long_start, _ = scalars(lengths_ref, None, most)
    half = ROPE // 2
    token = lax.broadcasted_iota(jnp.int32, (1, tokens), 1)
    position = jnp.zeros((1, tokens), jnp.int32)
    for r in range(lengths_ref.shape[0]):
        inside = (token >= starts[r]) & (token < starts[r] + lengths_ref[r])
        position = jnp.where(inside, device * lengths_ref[r] + token - starts[r], position)
    index = lax.broadcasted_iota(jnp.int32, (half, 1), 0)
    frequency = jnp.zeros((half, 1), jnp.float32)
    for i in range(half):
        frequency = jnp.where(index == i, np.float32(10000.0 ** (-2.0 * i / ROPE)), frequency)
    sine, cosine = sin_cos(frequency * position.astype(jnp.float32))
    gain = jnp.transpose(jnp.broadcast_to(kv_gain_ref[...].astype(jnp.float32).reshape(1, KVL), (128, KVL)))
    row_gain = gain_ref[...].reshape(1, model)
    source = lax.broadcasted_iota(jnp.int32, (tokens, tokens), 0) + long_start
    source = jnp.where(source >= tokens, source - tokens, source)
    turn = (source == lax.broadcasted_iota(jnp.int32, (tokens, tokens), 1)).astype(jnp.bfloat16)

    squares = jnp.zeros((tokens, 128), jnp.float32)
    begin = 0
    for i, depth in enumerate(chunks):
        part = slice(begin, begin + depth)
        for copy in copies[i]:
            copy.wait()
        x = x_buf[:, part]
        product = lax.dot_general(w_buf[:, part], x * row_gain[:, part], NT, preferred_element_type=jnp.float32)
        if i == 0:
            acc[...] = product
        else:
            acc[...] += product
        for j in range(depth // 128):
            piece = x[:, j * 128 : (j + 1) * 128].astype(jnp.float32)
            squares = squares + piece * piece
        begin += depth
    mean = jnp.sum(jnp.transpose(squares), axis=0, keepdims=True) * np.float32(1.0 / model)
    scale = lax.rsqrt(mean + EPSILON)
    latent = acc[:KVL, :]
    latent_mean = jnp.sum(latent * latent, axis=0, keepdims=True) * (scale * scale) * np.float32(1.0 / KVL)
    latent = latent * (scale * lax.rsqrt(latent_mean + EPSILON)) * wide(gain, tokens)
    first = acc[KVL : KVL + half, :] * scale
    second = acc[KVL + half :, :] * scale
    columns = jnp.concatenate(
        [latent, first * cosine - second * sine, second * cosine + first * sine], axis=0
    ).astype(jnp.bfloat16)
    turned = lax.dot_general(turn, columns, NT, preferred_element_type=jnp.float32)
    long, short = packed_rows(turned[:most]), packed_rows(turned[most:])
    rows_ref[...] = jnp.concatenate([long, short], axis=0).astype(jnp.bfloat16)
    short_ref[...] = short.astype(jnp.bfloat16)


def packed_rows(rows):
    deep = rows.shape[0] // PACK
    rotary = [rows[i * deep : (i + 1) * deep, KVL:] for i in range(PACK)]
    return jnp.concatenate([rows[:, :KVL], jnp.concatenate(rotary, axis=1)], axis=0)


def unpacked(ref, begin, rows):
    deep = rows // PACK
    after = begin + rows
    rotary = [ref[after : after + deep, i * ROPE : (i + 1) * ROPE] for i in range(PACK)]
    return ref[begin:after, :], jnp.concatenate(rotary, axis=0)


def score(q_ref, latent, rotary):
    scores = lax.dot_general(q_ref[:, :KVL], latent, NT, preferred_element_type=jnp.float32)
    return (scores + lax.dot_general(q_ref[:, KVL:], rotary, NT, preferred_element_type=jnp.float32)) * SCALE


def pick_kernel(most, sizes, lengths_ref, owners_ref, queries_hbm, long_ref, short_ref, mask_ref, order_ref, buf, long_buf, short_buf, sem):
    zs, xs, cores = sizes
    device = lax.axis_index("ctx")
    starts, long_start, long_block = scalars(lengths_ref, owners_ref, most)
    count, steps, _, heads = queries_hbm.shape
    local = heads // (zs * xs * cores)
    core = lax.rem(device, cores)
    here_x = lax.rem(device // cores, xs)
    here_z = device // (cores * xs)
    blocks = [long_block] + [jnp.where(long_block <= i, i + 1, i) for i in range(count - 1)]
    copies = [
        pltpu.make_async_copy(queries_hbm.at[block], buf.at[i], sem.at[i]) for i, block in enumerate(blocks)
    ]
    for copy in copies:
        copy.start()

    def head_of(rows, spread):
        row = lax.broadcasted_iota(jnp.int32, (rows, heads), 0)
        unit, inner = row // local, lax.rem(row, local)
        z = lax.rem(lax.rem(unit, zs) + here_z, zs)
        x = lax.rem(unit // zs + here_x, xs) if spread else here_x
        head = ((z * xs + x) * cores + core) * local + inner
        return (head == lax.broadcasted_iota(jnp.int32, (rows, heads), 1)).astype(jnp.bfloat16)

    long_pick, short_pick = head_of(xs * zs * local, True), head_of(zs * local, False)
    shape = mask_ref.shape
    local_row = lax.broadcasted_iota(jnp.int32, shape, 1) + (long_start + most)
    local_row = jnp.where(local_row >= shape[1] + most, local_row - (shape[1] + most), local_row)
    slot = lax.broadcasted_iota(jnp.int32, shape, 0) // (steps * local)
    mask = jnp.zeros(shape, jnp.float32)
    for i, (_, start, length) in enumerate(short_slots(lengths_ref, owners_ref, starts, long_block)):
        inside = (slot == i) & (local_row >= start) & (local_row < start + length)
        mask = jnp.where(inside, 1.0, mask)
    mask_ref[...] = mask
    row = lax.broadcasted_iota(jnp.int32, order_ref.shape, 0)
    marked = (row == long_block) | ((row >= count) & (row - count > long_block))
    order_ref[...] = jnp.where(marked, 1.0, 0.0)
    copies[0].wait()
    for t in range(steps):
        rows = lax.dot_general(long_pick, buf[0, t], NT, preferred_element_type=jnp.float32)
        for u in range(xs * zs):
            long_buf[(u * steps + t) * local : (u * steps + t + 1) * local, :] = rows[u * local : (u + 1) * local]
    long_ref[...] = long_buf[...].astype(jnp.bfloat16)
    for i in range(1, count):
        copies[i].wait()
        for t in range(steps):
            rows = lax.dot_general(short_pick, buf[i, t], NT, preferred_element_type=jnp.float32)
            for u in range(zs):
                at = ((u * (count - 1) + i - 1) * steps + t) * local
                short_buf[at : at + local, :] = rows[u * local : (u + 1) * local]
    short_ref[...] = short_buf[...].astype(jnp.bfloat16)


def as_line(column):
    return jnp.transpose(jnp.broadcast_to(column, (column.shape[0], 128)))[:8]


def as_columns(line):
    return jnp.transpose(jnp.broadcast_to(line, (128, line.shape[1])))


def stat_rows(line):
    rows = line.shape[1]
    high = line.astype(jnp.bfloat16).astype(jnp.float32)
    rest = line - high
    middle = rest.astype(jnp.bfloat16).astype(jnp.float32)
    low = rest - middle
    index = lax.broadcasted_iota(jnp.int32, (STAT_ROWS, rows), 0)
    pieces = jnp.where(index == 0, high, jnp.where(index == 1, middle, jnp.where(index == 2, low, 0.0)))
    if rows < KVL:
        pieces = jnp.concatenate([pieces, jnp.zeros((STAT_ROWS, KVL - rows), jnp.float32)], axis=1)
    return pieces


def read_line(pieces, rows):
    return pieces[0:1, :rows] + pieces[1:2, :rows] + pieces[2:3, :rows]


def wide(stat, width=KVL):
    return jnp.concatenate([stat] * (width // 128), axis=1)


def long_kernel(most, q_ref, key_refs, out_refs):
    keys = [unpacked(ref, 0, most) for ref in key_refs]
    latent, rotary = (jnp.concatenate(part, axis=0) for part in zip(*keys))
    rows = q_ref.shape[0] // len(out_refs)
    scores = score(q_ref, latent, rotary)
    peak = jnp.max(scores, axis=1, keepdims=True)
    weights = jnp.exp(scores - peak)
    total = jnp.sum(weights, axis=1, keepdims=True)
    mixed = jnp.dot(weights.astype(jnp.bfloat16), latent, preferred_element_type=jnp.float32) / total
    lse = peak + jnp.log(total)
    for j, ref in enumerate(out_refs):
        part = slice(j * rows, (j + 1) * rows)
        ref[...] = jnp.concatenate([mixed[part], stat_rows(as_line(lse[part]))], axis=0).astype(jnp.bfloat16)


def short_kernel(most, q_ref, mask_ref, row_refs, packed_refs, out_refs, lse_ref):
    tokens = row_refs[0].shape[0] * PACK // (PACK + 1)
    shorts = tokens - most
    begin = most + most // PACK
    keys = [unpacked(ref, begin, shorts) for ref in row_refs] + [unpacked(ref, 0, shorts) for ref in packed_refs]
    latent, rotary = (jnp.concatenate(part, axis=0) for part in zip(*keys))
    per_dest = mask_ref.shape[0]
    scores = score(q_ref, latent, rotary)
    allowed = jnp.concatenate([mask_ref[...]] * len(keys), axis=1)
    allowed = jnp.concatenate([allowed] * len(out_refs), axis=0) > 0.0
    scores = jnp.where(allowed, scores, -1e30)
    peak = jnp.max(scores, axis=1, keepdims=True)
    weights = jnp.where(allowed, jnp.exp(scores - peak), 0.0)
    total = jnp.sum(weights, axis=1, keepdims=True)
    mixed = jnp.dot(weights.astype(jnp.bfloat16), latent, preferred_element_type=jnp.float32) / total
    lse = peak + jnp.log(total)
    for k, ref in enumerate(out_refs):
        part = slice(k * per_dest, (k + 1) * per_dest)
        ref[...] = mixed[part].astype(jnp.bfloat16)
        lse_ref[k] = as_line(lse[part])


def merge_kernel(part_refs, lse_ref, out_refs):
    rows = part_refs[0].shape[0] - STAT_ROWS
    per_dest = rows // len(out_refs)
    parts = [ref[...].astype(jnp.float32) for ref in part_refs]
    lines = [read_line(part[rows:], rows) for part in parts]
    top = functools.reduce(jnp.maximum, lines)
    shares = [jnp.exp(line - top) for line in lines]
    whole = functools.reduce(lambda a, b: a + b, shares)
    mixed = functools.reduce(
        lambda a, b: a + b, [wide(as_columns(share / whole)) * part[:rows] for share, part in zip(shares, parts)]
    )
    lse = jnp.broadcast_to(top + jnp.log(whole), (8, rows))
    for k, ref in enumerate(out_refs):
        part = slice(k * per_dest, (k + 1) * per_dest)
        both = jnp.concatenate([lse_ref[k], lse[:, part]], axis=1)
        ref[...] = jnp.concatenate([mixed[part], stat_rows(both)], axis=0).astype(jnp.bfloat16)


def step_kernel(most, steps, lengths_ref, owners_ref, long_q_ref, short_q_ref, step_ref, after_ref, out_ref, lse_ref):
    count = lengths_ref.shape[0]
    _, _, long_block = scalars(lengths_ref, owners_ref, most)
    blocks = [jnp.where(long_block <= i, i + 1, i) for i in range(count - 1)] + [long_block]
    rows = out_ref.shape[0]
    per_slot = rows // count
    heads = per_slot // steps
    query = jnp.concatenate(
        [short_q_ref[: rows - per_slot, :].astype(jnp.float32), long_q_ref[:per_slot, :].astype(jnp.float32)], axis=0
    ).astype(jnp.bfloat16)
    keys = jnp.concatenate([step_ref[b].astype(jnp.float32) for b in blocks], axis=0).astype(jnp.bfloat16)
    scores = lax.dot_general(query, keys, NT, preferred_element_type=jnp.float32) * SCALE
    row = lax.broadcasted_iota(jnp.int32, scores.shape, 0)
    column = lax.broadcasted_iota(jnp.int32, scores.shape, 1)
    allowed = (row // per_slot == column // steps) & (lax.rem(column, steps) <= lax.rem(row, per_slot) // heads)
    scores = jnp.where(allowed, scores, -1e30)
    peak = jnp.max(scores, axis=1, keepdims=True)
    weights = jnp.where(allowed, jnp.exp(scores - peak), 0.0)
    total = jnp.sum(weights, axis=1, keepdims=True)
    out_ref[...] = jnp.dot(weights.astype(jnp.bfloat16), keys[:, :KVL], preferred_element_type=jnp.float32) / total
    lse_ref[...] = as_line(peak + jnp.log(total))


def last_kernel(order_ref, step_ref, step_lse_ref, short_refs, long_refs, out_ref):
    count = out_ref.shape[0]
    rows, per_slot = step_ref.shape[0], long_refs[0].shape[0] - STAT_ROWS
    shorts = rows - per_slot
    longs = [ref[...].astype(jnp.float32) for ref in long_refs]
    lines = [step_lse_ref[:1]] + [read_line(part[per_slot:], rows) for part in longs]
    top = functools.reduce(jnp.maximum, lines)
    shares = [jnp.exp(line - top) for line in lines]
    whole = functools.reduce(lambda a, b: a + b, shares)
    columns = [wide(as_columns(share / whole)) for share in shares]
    step = step_ref[...]
    short, long = columns[0][:shorts] * step[:shorts], columns[0][shorts:] * step[shorts:]
    for column, ref, part in zip(columns[1:], short_refs, longs):
        short = short + column[:shorts] * ref[...].astype(jnp.float32)
        long = long + column[shorts:] * part[:per_slot]
    slots = [short[i * per_slot : (i + 1) * per_slot] for i in range(count - 1)]
    order = order_ref[...]
    for b in range(count):
        is_long, behind = wide(order[b : b + 1]) > 0.0, wide(order[count + b : count + b + 1]) > 0.0
        block = jnp.where(behind, slots[max(b - 1, 0)], slots[min(b, count - 2)])
        out_ref[b] = jnp.where(is_long, long, block).astype(jnp.bfloat16)


SMEM = pl.BlockSpec(memory_space=pltpu.SMEM)
VMEM = pl.BlockSpec(memory_space=pltpu.VMEM)
HBM = pl.BlockSpec(memory_space=pl.ANY)


def params(**more):
    return pltpu.CompilerParams(vmem_limit_bytes=VMEM_BYTES, **more)


def shards(hidden, attn_gain, w_dkv, kv_gain, lengths, owners, queries, step_rows):
    devices = lax.axis_size("ctx")
    sizes = place(devices)
    zs, xs, cores = sizes
    tokens, model = hidden.shape
    count, steps, heads, _ = queries.shape
    most = min(3 * tokens // count, tokens - count + 1)
    shorts = tokens - most
    local = heads // devices
    bf16, f32 = jnp.bfloat16, jnp.float32

    def send(value, by_z=0, by_x=0, by_core=0):
        def device(z, x, c):
            return (z % zs * xs + x % xs) * cores + c % cores

        pairs = [
            (device(z, x, c), device(z + by_z, x + by_x, c + by_core))
            for z in range(zs)
            for x in range(xs)
            for c in range(cores)
        ]
        return lax.ppermute(value, "ctx", pairs)

    chunks = [1024] * ((model - 1024) // 1024)
    while sum(chunks) < model:
        chunks.append(min(512, model - sum(chunks)))
    row_keys, short_keys = pl.pallas_call(
        functools.partial(compress_kernel, most, chunks),
        in_specs=[HBM] * 5,
        out_specs=[VMEM, VMEM],
        out_shape=[
            jax.ShapeDtypeStruct((tokens + tokens // PACK, KVL), bf16),
            jax.ShapeDtypeStruct((shorts + shorts // PACK, KVL), bf16),
        ],
        scratch_shapes=[
            pltpu.VMEM((tokens, model), bf16),
            pltpu.VMEM((WIDTH, model), bf16),
            pltpu.VMEM((WIDTH, tokens), f32),
            pltpu.SMEM(lengths.shape, lengths.dtype),
            pltpu.VMEM(attn_gain.shape, bf16),
            pltpu.VMEM(kv_gain.shape, bf16),
            pltpu.SemaphoreType.DMA((3,)),
            pltpu.SemaphoreType.DMA((2, len(chunks))),
        ],
        compiler_params=params(),
        cost_estimate=pl.CostEstimate(
            flops=2 * tokens * model * WIDTH, bytes_accessed=2 * model * (tokens + WIDTH), transcendentals=0
        ),
        name="compress",
    )(*[pltpu.with_memory_space_constraint(v, pltpu.HBM) for v in (lengths, hidden, attn_gain, w_dkv.T, kv_gain)])

    long_rows, short_rows = zs * xs * steps * local, zs * (count - 1) * steps * local
    long_q, short_q, mask, order = pl.pallas_call(
        functools.partial(pick_kernel, most, sizes),
        in_specs=[SMEM, SMEM, HBM],
        out_specs=[VMEM] * 4,
        out_shape=[
            jax.ShapeDtypeStruct((long_rows, WIDTH), bf16),
            jax.ShapeDtypeStruct((short_rows, WIDTH), bf16),
            jax.ShapeDtypeStruct((short_rows // zs, shorts), f32),
            jax.ShapeDtypeStruct((2 * count, 128), f32),
        ],
        scratch_shapes=[
            pltpu.VMEM((count, steps, WIDTH, heads), bf16),
            pltpu.VMEM((long_rows, WIDTH), f32),
            pltpu.VMEM((short_rows, WIDTH), f32),
            pltpu.SemaphoreType.DMA((count,)),
        ],
        compiler_params=params(),
        cost_estimate=pl.CostEstimate(
            flops=2 * (long_rows + short_rows) * WIDTH * heads,
            bytes_accessed=2 * count * steps * WIDTH * heads,
            transcendentals=0,
        ),
        name="pick_queries",
    )(lengths, owners, queries.transpose(0, 1, 3, 2))

    short_in = [send(short_keys, by_x=j) for j in range(1, xs)]
    row_in = [row_keys] + [send(row_keys, by_core=j) for j in range(1, cores)]

    x_rows = long_rows // xs + STAT_ROWS
    parts = pl.pallas_call(
        lambda q, *refs: long_kernel(most, q, refs[:cores], refs[cores:]),
        in_specs=[VMEM] * (1 + cores),
        out_specs=[VMEM] * xs,
        out_shape=[jax.ShapeDtypeStruct((x_rows, KVL), bf16)] * xs,
        compiler_params=params(),
        cost_estimate=pl.CostEstimate(
            flops=2 * long_rows * most * cores * (WIDTH + KVL), bytes_accessed=4 * most * WIDTH, transcendentals=0
        ),
        name="long_part",
    )(long_q, *row_in)
    sent = [send(parts[j], by_x=j) for j in range(1, xs)]
    own, *short_in = lax.optimization_barrier((parts[0], *short_in))
    parts = [own] + sent
    short_in = short_in + [send(k, by_core=j) for j in range(1, cores) for k in short_in]

    per_short, per_long = short_rows // zs, long_rows // xs // zs
    ins = cores + len(short_in)
    *short_parts, short_lse = pl.pallas_call(
        lambda q, m, *refs: short_kernel(most, q, m, refs[:cores], refs[cores:ins], refs[ins : ins + zs], refs[-1]),
        in_specs=[VMEM] * (2 + ins),
        out_specs=[VMEM] * (zs + 1),
        out_shape=[jax.ShapeDtypeStruct((per_short, KVL), bf16)] * zs + [jax.ShapeDtypeStruct((zs, 8, per_short), f32)],
        compiler_params=params(),
        cost_estimate=pl.CostEstimate(
            flops=2 * short_rows * shorts * ins * (WIDTH + KVL), bytes_accessed=4 * shorts * ins * WIDTH, transcendentals=0
        ),
        name="short_part",
    )(short_q, mask, *row_in, *short_in)
    short_parts = [short_parts[0]] + [send(short_parts[k], by_z=k) for k in range(1, zs)]

    long_parts = pl.pallas_call(
        lambda *refs: merge_kernel(refs[:xs], refs[xs], refs[xs + 1 :]),
        in_specs=[VMEM] * (xs + 1),
        out_specs=[VMEM] * zs,
        out_shape=[jax.ShapeDtypeStruct((per_long + STAT_ROWS, KVL), bf16)] * zs,
        compiler_params=params(),
        cost_estimate=pl.CostEstimate(flops=0, bytes_accessed=2 * xs * x_rows * KVL, transcendentals=0),
        name="long_merge",
    )(*parts, short_lse)
    after = short_parts[1] if zs > 1 else long_parts[0]

    rows = per_short + per_long
    step_part, step_lse = pl.pallas_call(
        functools.partial(step_kernel, most, steps),
        in_specs=[SMEM, SMEM, VMEM, VMEM, VMEM, HBM],
        out_specs=[VMEM, VMEM],
        out_shape=[jax.ShapeDtypeStruct((rows, KVL), f32), jax.ShapeDtypeStruct((8, rows), f32)],
        compiler_params=params(),
        cost_estimate=pl.CostEstimate(flops=0, bytes_accessed=4 * rows * KVL, transcendentals=0),
        name="step_part",
    )(lengths, owners, long_q, short_q, step_rows, after)

    step_part, *late = lax.optimization_barrier((step_part, *long_parts[3:]))
    long_parts = [*long_parts[:3], *late]
    long_parts = [long_parts[0]] + [send(long_parts[k], by_z=k) for k in range(1, zs)]

    out = pl.pallas_call(
        lambda o, s, l, *refs: last_kernel(o, s, l, refs[:zs], refs[zs : 2 * zs], refs[2 * zs]),
        in_specs=[VMEM] * (3 + 2 * zs),
        out_specs=VMEM,
        out_shape=jax.ShapeDtypeStruct((count, steps * local, KVL), bf16),
        compiler_params=params(),
        cost_estimate=pl.CostEstimate(flops=0, bytes_accessed=2 * zs * rows * KVL, transcendentals=0),
        name="combine",
    )(order, step_part, step_lse, *short_parts, *long_parts)
    return out.reshape(count, steps, local, KVL)


def solution(mesh):
    in_specs = (
        P(("groups", "ctx"), None),
        P(),
        P(),
        P(),
        P("groups"),
        P("groups"),
        P("groups", None, None, None),
        P("groups", None, None),
    )
    out_specs = P("groups", None, "ctx", None)
    return jax.shard_map(shards, mesh=mesh, in_specs=in_specs, out_specs=out_specs, check_vma=False)
```

```python
import functools
import math

import jax
import jax.numpy as jnp
import numpy as np
from jax import lax
from jax.experimental import pallas as pl
from jax.experimental.pallas import tpu as pltpu
from jax.sharding import PartitionSpec as P

KVL = 512
ROPE = 64
NOPE = 128
WIDTH = KVL + ROPE
EPSILON = 1e-06
SCALE = (NOPE + ROPE) ** (-0.5)
STAT_ROWS = 8
PACK = KVL // ROPE
VMEM_BYTES = 48 * 1024 * 1024

NT = (((1,), (1,)), ((), ()))


def place(devices):
    cores = 2 if devices % 2 == 0 else 1
    chips = devices // cores
    along_x = max(k for k in range(1, chips + 1) if chips % k == 0 and k * k * k <= chips)
    return chips // along_x, along_x, cores


def shifted(z, by, zs):
    if zs & (zs - 1) == 0:
        return z ^ by
    return (z + by) % zs


def scalars(lengths_ref, owners_ref, most):
    count = lengths_ref.shape[0]
    starts = []
    total = jnp.int32(0)
    for r in range(count):
        starts.append(total)
        total = total + lengths_ref[r]
    long_start, long_block = jnp.int32(0), jnp.int32(0)
    for r in range(count):
        is_long = lengths_ref[r] == most
        long_start = jnp.where(is_long, starts[r], long_start)
        if owners_ref is not None:
            long_block = jnp.where(is_long, owners_ref[r], long_block)
    return starts, long_start, long_block


def short_slots(lengths_ref, owners_ref, starts, long_block):
    count = lengths_ref.shape[0]
    slots = []
    for i in range(count - 1):
        block = jnp.where(long_block <= i, jnp.int32(i + 1), jnp.int32(i))
        first, rows = jnp.int32(0), jnp.int32(0)
        for r in range(count):
            is_it = owners_ref[r] == block
            first = jnp.where(is_it, starts[r], first)
            rows = jnp.where(is_it, lengths_ref[r], rows)
        slots.append((block, first, rows))
    return slots


def sin_cos(angle):
    n = jnp.round(angle * np.float32(2.0 / math.pi))
    r = ((angle - n * np.float32(1.5703125)) - n * np.float32(4.8375129699707031e-4)) - n * np.float32(
        7.5497899548918822e-8
    )
    z = r * r
    sine = ((np.float32(-1.9515295891e-4) * z + np.float32(8.3321608736e-3)) * z + np.float32(-1.6666654611e-1)) * z * r + r
    cosine = (
        ((np.float32(2.443315711809948e-5) * z + np.float32(-1.388731625493765e-3)) * z + np.float32(4.166664568298827e-2)) * z * z
        - np.float32(0.5) * z
        + np.float32(1.0)
    )
    quadrant = n.astype(jnp.int32) & 3
    odd = (quadrant & 1) == 1
    out_sine = jnp.where(odd, cosine, sine)
    out_cosine = jnp.where(odd, sine, cosine)
    out_sine = jnp.where(quadrant >= 2, -out_sine, out_sine)
    out_cosine = jnp.where((quadrant == 1) | (quadrant == 2), -out_cosine, out_cosine)
    return out_sine, out_cosine


def compress_kernel(
    most,
    chunks,
    lengths_hbm,
    x_hbm,
    gain_hbm,
    w_hbm,
    kv_gain_hbm,
    rows_ref,
    short_ref,
    x_buf,
    w_buf,
    acc,
    lengths_ref,
    gain_ref,
    kv_gain_ref,
    small,
    sem,
):
    tokens, model = x_buf.shape
    head = [
        pltpu.make_async_copy(source, target, small.at[i])
        for i, (source, target) in enumerate(
            ((lengths_hbm, lengths_ref), (gain_hbm, gain_ref), (kv_gain_hbm, kv_gain_ref))
        )
    ]
    copies, begin = [], 0
    for i, depth in enumerate(chunks):
        part = pl.ds(begin, depth)
        copies.append(
            (
                pltpu.make_async_copy(w_hbm.at[:, part], w_buf.at[:, part], sem.at[0, i]),
                pltpu.make_async_copy(x_hbm.at[:, part], x_buf.at[:, part], sem.at[1, i]),
            )
        )
        begin += depth
    for copy in head:
        copy.start()
    for copy in copies[0] + copies[1]:
        copy.start()
    for copy in head:
        copy.wait()
    for pair in copies[2:]:
        for copy in pair:
            copy.start()

    device = lax.axis_index("ctx")
    starts, long_start, _ = scalars(lengths_ref, None, most)
    half = ROPE // 2
    token = lax.broadcasted_iota(jnp.int32, (1, tokens), 1)
    position = jnp.zeros((1, tokens), jnp.int32)
    for r in range(lengths_ref.shape[0]):
        inside = (token >= starts[r]) & (token < starts[r] + lengths_ref[r])
        position = jnp.where(inside, device * lengths_ref[r] + token - starts[r], position)
    index = lax.broadcasted_iota(jnp.int32, (half, 1), 0)
    frequency = jnp.zeros((half, 1), jnp.float32)
    for i in range(half):
        frequency = jnp.where(index == i, np.float32(10000.0 ** (-2.0 * i / ROPE)), frequency)
    sine, cosine = sin_cos(frequency * position.astype(jnp.float32))
    gain = jnp.transpose(jnp.broadcast_to(kv_gain_ref[...].astype(jnp.float32).reshape(1, KVL), (128, KVL)))
    row_gain = gain_ref[...].reshape(1, model)
    source = lax.broadcasted_iota(jnp.int32, (tokens, tokens), 0) + long_start
    source = jnp.where(source >= tokens, source - tokens, source)
    turn = (source == lax.broadcasted_iota(jnp.int32, (tokens, tokens), 1)).astype(jnp.bfloat16)

    squares = jnp.zeros((tokens, 128), jnp.float32)
    begin = 0
    for i, depth in enumerate(chunks):
        part = slice(begin, begin + depth)
        for copy in copies[i]:
            copy.wait()
        x = x_buf[:, part]
        product = lax.dot_general(w_buf[:, part], x * row_gain[:, part], NT, preferred_element_type=jnp.float32)
        if i == 0:
            acc[...] = product
        else:
            acc[...] += product
        for j in range(depth // 128):
            piece = x[:, j * 128 : (j + 1) * 128].astype(jnp.float32)
            squares = squares + piece * piece
        begin += depth
    mean = jnp.sum(jnp.transpose(squares), axis=0, keepdims=True) * np.float32(1.0 / model)
    scale = lax.rsqrt(mean + EPSILON)
    latent = acc[:KVL, :]
    latent_mean = jnp.sum(latent * latent, axis=0, keepdims=True) * (scale * scale) * np.float32(1.0 / KVL)
    latent = latent * (scale * lax.rsqrt(latent_mean + EPSILON)) * wide(gain, tokens)
    first = acc[KVL : KVL + half, :] * scale
    second = acc[KVL + half :, :] * scale
    columns = jnp.concatenate(
        [latent, first * cosine - second * sine, second * cosine + first * sine], axis=0
    ).astype(jnp.bfloat16)
    turned = lax.dot_general(turn, columns, NT, preferred_element_type=jnp.float32)
    long, short = packed_rows(turned[:most]), packed_rows(turned[most:])
    rows_ref[...] = jnp.concatenate([long, short], axis=0).astype(jnp.bfloat16)
    short_ref[...] = short.astype(jnp.bfloat16)


def packed_rows(rows):
    deep = rows.shape[0] // PACK
    rotary = [rows[i * deep : (i + 1) * deep, KVL:] for i in range(PACK)]
    return jnp.concatenate([rows[:, :KVL], jnp.concatenate(rotary, axis=1)], axis=0)


def unpacked(ref, begin, rows):
    deep = rows // PACK
    after = begin + rows
    rotary = [ref[after : after + deep, i * ROPE : (i + 1) * ROPE] for i in range(PACK)]
    return ref[begin:after, :], jnp.concatenate(rotary, axis=0)


def score(q_ref, latent, rotary):
    scores = lax.dot_general(q_ref[:, :KVL], latent, NT, preferred_element_type=jnp.float32)
    return (scores + lax.dot_general(q_ref[:, KVL:], rotary, NT, preferred_element_type=jnp.float32)) * SCALE


def pick_kernel(most, sizes, lengths_ref, owners_ref, queries_hbm, long_ref, short_ref, mask_ref, order_ref, buf, long_buf, short_buf, sem):
    zs, xs, cores = sizes
    device = lax.axis_index("ctx")
    starts, long_start, long_block = scalars(lengths_ref, owners_ref, most)
    count, steps, _, heads = queries_hbm.shape
    local = heads // (zs * xs * cores)
    core = lax.rem(device, cores)
    here_x = lax.rem(device // cores, xs)
    here_z = device // (cores * xs)
    blocks = [long_block] + [jnp.where(long_block <= i, i + 1, i) for i in range(count - 1)]
    copies = [
        pltpu.make_async_copy(queries_hbm.at[block], buf.at[i], sem.at[i]) for i, block in enumerate(blocks)
    ]
    for copy in copies:
        copy.start()

    def head_of(rows, spread):
        row = lax.broadcasted_iota(jnp.int32, (rows, heads), 0)
        unit, inner = row // local, lax.rem(row, local)
        z = shifted(here_z, lax.rem(unit, zs), zs)
        x = lax.rem(unit // zs + here_x, xs) if spread else here_x
        head = ((z * xs + x) * cores + core) * local + inner
        return (head == lax.broadcasted_iota(jnp.int32, (rows, heads), 1)).astype(jnp.bfloat16)

    long_pick, short_pick = head_of(xs * zs * local, True), head_of(zs * local, False)
    shape = mask_ref.shape
    local_row = lax.broadcasted_iota(jnp.int32, shape, 1) + (long_start + most)
    local_row = jnp.where(local_row >= shape[1] + most, local_row - (shape[1] + most), local_row)
    slot = lax.broadcasted_iota(jnp.int32, shape, 0) // (steps * local)
    mask = jnp.zeros(shape, jnp.float32)
    for i, (_, start, length) in enumerate(short_slots(lengths_ref, owners_ref, starts, long_block)):
        inside = (slot == i) & (local_row >= start) & (local_row < start + length)
        mask = jnp.where(inside, 1.0, mask)
    mask_ref[...] = mask
    row = lax.broadcasted_iota(jnp.int32, order_ref.shape, 0)
    marked = (row == long_block) | ((row >= count) & (row - count > long_block))
    order_ref[...] = jnp.where(marked, 1.0, 0.0)
    copies[0].wait()
    for t in range(steps):
        rows = lax.dot_general(long_pick, buf[0, t], NT, preferred_element_type=jnp.float32)
        for u in range(xs * zs):
            long_buf[(u * steps + t) * local : (u * steps + t + 1) * local, :] = rows[u * local : (u + 1) * local]
    long_ref[...] = long_buf[...].astype(jnp.bfloat16)
    for i in range(1, count):
        copies[i].wait()
        for t in range(steps):
            rows = lax.dot_general(short_pick, buf[i, t], NT, preferred_element_type=jnp.float32)
            for u in range(zs):
                at = ((u * (count - 1) + i - 1) * steps + t) * local
                short_buf[at : at + local, :] = rows[u * local : (u + 1) * local]
    short_ref[...] = short_buf[...].astype(jnp.bfloat16)


def as_line(column):
    return jnp.transpose(jnp.broadcast_to(column, (column.shape[0], 128)))[:8]


def as_columns(line):
    return jnp.transpose(jnp.broadcast_to(line, (128, line.shape[1])))


def stat_rows(line):
    rows = line.shape[1]
    high = line.astype(jnp.bfloat16).astype(jnp.float32)
    rest = line - high
    middle = rest.astype(jnp.bfloat16).astype(jnp.float32)
    low = rest - middle
    index = lax.broadcasted_iota(jnp.int32, (STAT_ROWS, rows), 0)
    pieces = jnp.where(index == 0, high, jnp.where(index == 1, middle, jnp.where(index == 2, low, 0.0)))
    if rows < KVL:
        pieces = jnp.concatenate([pieces, jnp.zeros((STAT_ROWS, KVL - rows), jnp.float32)], axis=1)
    return pieces


def read_line(pieces, rows):
    return pieces[0:1, :rows] + pieces[1:2, :rows] + pieces[2:3, :rows]


def wide(stat, width=KVL):
    return jnp.concatenate([stat] * (width // 128), axis=1)


def long_kernel(most, q_ref, key_refs, out_refs):
    keys = [unpacked(ref, 0, most) for ref in key_refs]
    latent, rotary = (jnp.concatenate(part, axis=0) for part in zip(*keys))
    rows = q_ref.shape[0] // len(out_refs)
    scores = score(q_ref, latent, rotary)
    peak = jnp.max(scores, axis=1, keepdims=True)
    weights = jnp.exp(scores - peak)
    total = jnp.sum(weights, axis=1, keepdims=True)
    mixed = jnp.dot(weights.astype(jnp.bfloat16), latent, preferred_element_type=jnp.float32) / total
    lse = peak + jnp.log(total)
    for j, ref in enumerate(out_refs):
        part = slice(j * rows, (j + 1) * rows)
        ref[...] = jnp.concatenate([mixed[part], stat_rows(as_line(lse[part]))], axis=0).astype(jnp.bfloat16)


def short_kernel(most, q_ref, mask_ref, row_refs, packed_refs, out_refs, lse_ref):
    tokens = row_refs[0].shape[0] * PACK // (PACK + 1)
    shorts = tokens - most
    begin = most + most // PACK
    keys = [unpacked(ref, begin, shorts) for ref in row_refs] + [unpacked(ref, 0, shorts) for ref in packed_refs]
    latent, rotary = (jnp.concatenate(part, axis=0) for part in zip(*keys))
    per_dest = mask_ref.shape[0]
    scores = score(q_ref, latent, rotary)
    allowed = jnp.concatenate([mask_ref[...]] * len(keys), axis=1)
    allowed = jnp.concatenate([allowed] * len(out_refs), axis=0) > 0.0
    scores = jnp.where(allowed, scores, -1e30)
    peak = jnp.max(scores, axis=1, keepdims=True)
    weights = jnp.where(allowed, jnp.exp(scores - peak), 0.0)
    total = jnp.sum(weights, axis=1, keepdims=True)
    mixed = jnp.dot(weights.astype(jnp.bfloat16), latent, preferred_element_type=jnp.float32) / total
    lse = peak + jnp.log(total)
    for k, ref in enumerate(out_refs):
        part = slice(k * per_dest, (k + 1) * per_dest)
        ref[...] = mixed[part].astype(jnp.bfloat16)
        lse_ref[k] = as_line(lse[part])


def merge_kernel(part_refs, lse_ref, out_refs):
    rows = part_refs[0].shape[0] - STAT_ROWS
    per_dest = rows // len(out_refs)
    parts = [ref[...].astype(jnp.float32) for ref in part_refs]
    lines = [read_line(part[rows:], rows) for part in parts]
    top = functools.reduce(jnp.maximum, lines)
    shares = [jnp.exp(line - top) for line in lines]
    whole = functools.reduce(lambda a, b: a + b, shares)
    mixed = functools.reduce(
        lambda a, b: a + b, [wide(as_columns(share / whole)) * part[:rows] for share, part in zip(shares, parts)]
    )
    lse = jnp.broadcast_to(top + jnp.log(whole), (8, rows))
    for k, ref in enumerate(out_refs):
        part = slice(k * per_dest, (k + 1) * per_dest)
        both = jnp.concatenate([lse_ref[k], lse[:, part]], axis=1)
        ref[...] = jnp.concatenate([mixed[part], stat_rows(both)], axis=0).astype(jnp.bfloat16)


def step_kernel(
    most, steps, lengths_ref, owners_ref, long_q_ref, short_q_ref, step_ref, short_ref, long_ref, out_ref, lse_ref
):
    count = lengths_ref.shape[0]
    _, _, long_block = scalars(lengths_ref, owners_ref, most)
    blocks = [jnp.where(long_block <= i, i + 1, i) for i in range(count - 1)] + [long_block]
    rows = out_ref.shape[0]
    per_slot = rows // count
    heads = per_slot // steps
    query = jnp.concatenate(
        [short_q_ref[: rows - per_slot, :].astype(jnp.float32), long_q_ref[:per_slot, :].astype(jnp.float32)], axis=0
    ).astype(jnp.bfloat16)
    keys = jnp.concatenate([step_ref[b].astype(jnp.float32) for b in blocks], axis=0).astype(jnp.bfloat16)
    scores = lax.dot_general(query, keys, NT, preferred_element_type=jnp.float32) * SCALE
    row = lax.broadcasted_iota(jnp.int32, scores.shape, 0)
    column = lax.broadcasted_iota(jnp.int32, scores.shape, 1)
    allowed = (row // per_slot == column // steps) & (lax.rem(column, steps) <= lax.rem(row, per_slot) // heads)
    scores = jnp.where(allowed, scores, -1e30)
    peak = jnp.max(scores, axis=1, keepdims=True)
    weights = jnp.where(allowed, jnp.exp(scores - peak), 0.0)
    total = jnp.sum(weights, axis=1, keepdims=True)
    mixed = jnp.dot(weights.astype(jnp.bfloat16), keys[:, :KVL], preferred_element_type=jnp.float32) / total
    line = as_line(peak + jnp.log(total))[:1]
    long = long_ref[...].astype(jnp.float32)
    own = jnp.concatenate([short_ref[...].astype(jnp.float32), long[:per_slot]], axis=0)
    own_line = read_line(long[per_slot:], rows)
    top = jnp.maximum(line, own_line)
    share, own_share = jnp.exp(line - top), jnp.exp(own_line - top)
    whole = share + own_share
    out_ref[...] = wide(as_columns(share / whole)) * mixed + wide(as_columns(own_share / whole)) * own
    lse_ref[...] = jnp.broadcast_to(top + jnp.log(whole), lse_ref.shape)


def last_kernel(order_ref, step_ref, step_lse_ref, short_refs, long_refs, out_ref):
    count = out_ref.shape[0]
    rows = step_ref.shape[0]
    per_slot = rows // count
    shorts = rows - per_slot
    longs = [ref[...].astype(jnp.float32) for ref in long_refs]
    lines = [step_lse_ref[:1]] + [read_line(part[per_slot:], rows) for part in longs]
    top = functools.reduce(jnp.maximum, lines)
    shares = [jnp.exp(line - top) for line in lines]
    whole = functools.reduce(lambda a, b: a + b, shares)
    columns = [wide(as_columns(share / whole)) for share in shares]
    step = step_ref[...]
    short, long = columns[0][:shorts] * step[:shorts], columns[0][shorts:] * step[shorts:]
    for column, ref, part in zip(columns[1:], short_refs, longs):
        short = short + column[:shorts] * ref[...].astype(jnp.float32)
        long = long + column[shorts:] * part[:per_slot]
    slots = [short[i * per_slot : (i + 1) * per_slot] for i in range(count - 1)]
    order = order_ref[...]
    for b in range(count):
        is_long, behind = wide(order[b : b + 1]) > 0.0, wide(order[count + b : count + b + 1]) > 0.0
        block = jnp.where(behind, slots[max(b - 1, 0)], slots[min(b, count - 2)])
        out_ref[b] = jnp.where(is_long, long, block).astype(jnp.bfloat16)


SMEM = pl.BlockSpec(memory_space=pltpu.SMEM)
VMEM = pl.BlockSpec(memory_space=pltpu.VMEM)
HBM = pl.BlockSpec(memory_space=pl.ANY)


def params(**more):
    return pltpu.CompilerParams(vmem_limit_bytes=VMEM_BYTES, **more)


def shards(hidden, attn_gain, w_dkv, kv_gain, lengths, owners, queries, step_rows):
    devices = lax.axis_size("ctx")
    sizes = place(devices)
    zs, xs, cores = sizes
    tokens, model = hidden.shape
    count, steps, heads, _ = queries.shape
    most = min(3 * tokens // count, tokens - count + 1)
    shorts = tokens - most
    local = heads // devices
    bf16, f32 = jnp.bfloat16, jnp.float32

    def send(value, by_z=0, by_x=0, by_core=0):
        def device(z, x, c):
            return (z * xs + x % xs) * cores + c % cores

        pairs = [
            (device(z, x, c), device(shifted(z, by_z, zs), x + by_x, c + by_core))
            for z in range(zs)
            for x in range(xs)
            for c in range(cores)
        ]
        return lax.ppermute(value, "ctx", pairs)

    chunks = [1024] * (model // 1024)
    if sum(chunks) < model:
        chunks.append(model - sum(chunks))
    row_keys, short_keys = pl.pallas_call(
        functools.partial(compress_kernel, most, chunks),
        in_specs=[HBM] * 5,
        out_specs=[VMEM, VMEM],
        out_shape=[
            jax.ShapeDtypeStruct((tokens + tokens // PACK, KVL), bf16),
            jax.ShapeDtypeStruct((shorts + shorts // PACK, KVL), bf16),
        ],
        scratch_shapes=[
            pltpu.VMEM((tokens, model), bf16),
            pltpu.VMEM((WIDTH, model), bf16),
            pltpu.VMEM((WIDTH, tokens), f32),
            pltpu.SMEM(lengths.shape, lengths.dtype),
            pltpu.VMEM(attn_gain.shape, bf16),
            pltpu.VMEM(kv_gain.shape, bf16),
            pltpu.SemaphoreType.DMA((3,)),
            pltpu.SemaphoreType.DMA((2, len(chunks))),
        ],
        compiler_params=params(),
        cost_estimate=pl.CostEstimate(
            flops=2 * tokens * model * WIDTH, bytes_accessed=2 * model * (tokens + WIDTH), transcendentals=0
        ),
        name="compress",
    )(*[pltpu.with_memory_space_constraint(v, pltpu.HBM) for v in (lengths, hidden, attn_gain, w_dkv.T, kv_gain)])

    long_rows, short_rows = zs * xs * steps * local, zs * (count - 1) * steps * local
    long_q, short_q, mask, order = pl.pallas_call(
        functools.partial(pick_kernel, most, sizes),
        in_specs=[SMEM, SMEM, HBM],
        out_specs=[VMEM] * 4,
        out_shape=[
            jax.ShapeDtypeStruct((long_rows, WIDTH), bf16),
            jax.ShapeDtypeStruct((short_rows, WIDTH), bf16),
            jax.ShapeDtypeStruct((short_rows // zs, shorts), f32),
            jax.ShapeDtypeStruct((2 * count, 128), f32),
        ],
        scratch_shapes=[
            pltpu.VMEM((count, steps, WIDTH, heads), bf16),
            pltpu.VMEM((long_rows, WIDTH), f32),
            pltpu.VMEM((short_rows, WIDTH), f32),
            pltpu.SemaphoreType.DMA((count,)),
        ],
        compiler_params=params(),
        cost_estimate=pl.CostEstimate(
            flops=2 * (long_rows + short_rows) * WIDTH * heads,
            bytes_accessed=2 * count * steps * WIDTH * heads,
            transcendentals=0,
        ),
        name="pick_queries",
    )(lengths, owners, pltpu.with_memory_space_constraint(queries.transpose(0, 1, 3, 2), pltpu.HBM))

    short_in = [send(short_keys, by_x=j) for j in range(1, xs)]
    row_in = [row_keys] + [send(row_keys, by_core=j) for j in range(1, cores)]

    x_rows = long_rows // xs + STAT_ROWS
    parts = pl.pallas_call(
        lambda q, *refs: long_kernel(most, q, refs[:cores], refs[cores:]),
        in_specs=[VMEM] * (1 + cores),
        out_specs=[VMEM] * xs,
        out_shape=[jax.ShapeDtypeStruct((x_rows, KVL), bf16)] * xs,
        compiler_params=params(),
        cost_estimate=pl.CostEstimate(
            flops=2 * long_rows * most * cores * (WIDTH + KVL), bytes_accessed=4 * most * WIDTH, transcendentals=0
        ),
        name="long_part",
    )(long_q, *row_in)
    sent = [send(parts[j], by_x=j) for j in range(1, xs)]
    own, *short_in = lax.optimization_barrier((parts[0], *short_in))
    parts = [own] + sent
    short_in = short_in + [send(k, by_core=j) for j in range(1, cores) for k in short_in]

    per_short, per_long = short_rows // zs, long_rows // xs // zs
    ins = cores + len(short_in)
    *short_parts, short_lse = pl.pallas_call(
        lambda q, m, *refs: short_kernel(most, q, m, refs[:cores], refs[cores:ins], refs[ins : ins + zs], refs[-1]),
        in_specs=[VMEM] * (2 + ins),
        out_specs=[VMEM] * (zs + 1),
        out_shape=[jax.ShapeDtypeStruct((per_short, KVL), bf16)] * zs + [jax.ShapeDtypeStruct((zs, 8, per_short), f32)],
        compiler_params=params(),
        cost_estimate=pl.CostEstimate(
            flops=2 * short_rows * shorts * ins * (WIDTH + KVL), bytes_accessed=4 * shorts * ins * WIDTH, transcendentals=0
        ),
        name="short_part",
    )(short_q, mask, *row_in, *short_in)
    turns = [*range(2, zs), 1] if zs > 1 else []
    came = {k: send(short_parts[k], by_z=k) for k in turns}
    short_parts = [came.get(k, part) for k, part in enumerate(short_parts)]

    long_parts = pl.pallas_call(
        lambda *refs: merge_kernel(refs[:xs], refs[xs], refs[xs + 1 :]),
        in_specs=[VMEM] * (xs + 1),
        out_specs=[VMEM] * zs,
        out_shape=[jax.ShapeDtypeStruct((per_long + STAT_ROWS, KVL), bf16)] * zs,
        compiler_params=params(),
        cost_estimate=pl.CostEstimate(flops=0, bytes_accessed=2 * xs * x_rows * KVL, transcendentals=0),
        name="long_merge",
    )(*parts, short_lse)

    rows = per_short + per_long
    step_part, step_lse = pl.pallas_call(
        functools.partial(step_kernel, most, steps),
        in_specs=[SMEM, SMEM] + [VMEM] * 5,
        out_specs=[VMEM, VMEM],
        out_shape=[jax.ShapeDtypeStruct((rows, KVL), f32), jax.ShapeDtypeStruct((8, rows), f32)],
        compiler_params=params(),
        cost_estimate=pl.CostEstimate(flops=0, bytes_accessed=4 * rows * KVL, transcendentals=0),
        name="step_part",
    )(lengths, owners, long_q, short_q, step_rows, short_parts[0], long_parts[0])

    late = turns[2:]
    tied = [long_parts[k] for k in late]
    if late:
        short_parts[turns[0]], *tied = lax.optimization_barrier((short_parts[turns[0]], *tied))
    ready = dict(zip(late, tied))
    came = {k: send(ready.get(k, long_parts[k]), by_z=k) for k in turns}
    long_parts = [came[k] for k in range(1, zs)]

    out = pl.pallas_call(
        lambda o, s, l, *refs: last_kernel(o, s, l, refs[: zs - 1], refs[zs - 1 : -1], refs[-1]),
        in_specs=[VMEM] * (1 + 2 * zs),
        out_specs=VMEM,
        out_shape=jax.ShapeDtypeStruct((count, steps * local, KVL), bf16),
        compiler_params=params(),
        cost_estimate=pl.CostEstimate(flops=0, bytes_accessed=2 * zs * rows * KVL, transcendentals=0),
        name="combine",
    )(order, step_part, step_lse, *short_parts[1:], *long_parts)
    return out.reshape(count, steps, local, KVL)


def solution(mesh):
    in_specs = (
        P(("groups", "ctx"), None),
        P(),
        P(),
        P(),
        P("groups"),
        P("groups"),
        P("groups", None, None, None),
        P("groups", None, None),
    )
    out_specs = P("groups", None, "ctx", None)
    return jax.shard_map(shards, mesh=mesh, in_specs=in_specs, out_specs=out_specs, check_vma=False)
```
